128 devices in a mesh: query: 8 (over z, core), passage: 16 (over y, x).
Axes of the slice: x: 4, y: 4, z: 4, core: 2. Of those that a mesh axis runs over, the one named last changes fastest.
Arguments:
- queries: bfloat16 [32768, 4096], P(('query', 'passage')), may hold values from -24 to 24
- passages: bfloat16 [8192, 4096], P('passage', 'query'), may hold values from -24 to 24
- lists: int32 [256, 8], P(('query', 'passage')), may hold values from -1 to 31, as said below
- positive: int32 [32768], P(('query', 'passage')), may hold values from 0 to 8191, as said below
Outputs:
- loss: float32 [32768], P(('query', 'passage'))
The draws below stay inside these ranges and needn't reach their ends.
Inputs may be any that keep to these rules, and one draw needn't show every extreme that they name: `lists`: each row holds distinct passage block ids in its first slots and -1 in the rest; at least 6 ids in every row, and row 0 fills all 8 slots; within each aligned group of 2 rows (the rows of one device) no two rows list blocks of the same owner, block id // 2. Query i's positive passage lies in block lists[i // 128, 0].
All inputs are finite; a program needn't handle non-finite values.
Results may differ from the reference program's by a relative error of at most 0.0003.
Values may be sent and summed in bfloat16 or wider, within the bound.
No kernel may reach another device: no remote copies, remote signals or barrier semaphores. Data moves between devices by JAX's collectives and lax.ppermute only.
A program may use at most 192 MiB of HBM per device.

```python
import jax
import jax.numpy as jnp
from jax import lax

D = 4096
QROWS = 128
PBLK = 256
PB_DEV = 2
QB_DEV = 2
LMAX = 8
QBLOCKS = 256
Q = 32768
NPB = 32
P_SIZE = 8192


def shuffle_owners(subkey):
    return jax.random.permutation(subkey, NPB // PB_DEV)


def listed_blocks(key):
    key_hot, key_noise, key_coin, key_count, key_split = jax.random.split(jax.random.fold_in(key, 11), 5)
    owners = NPB // PB_DEV
    groups = QBLOCKS // QB_DEV
    hot = jax.random.permutation(key_hot, NPB) < max(NPB // 8, 1)
    shuffled = jax.vmap(shuffle_owners)(jax.random.split(key_split, groups))
    position = jnp.arange(owners, dtype=jnp.int32)[None, :, None]
    owner_ids = jnp.arange(owners, dtype=jnp.int32)[None, None, :]
    assigned = jnp.sum(jnp.where(shuffled[:, :, None] == owner_ids, position % QB_DEV, 0), axis=1)
    assigned_rows = jnp.repeat(assigned, QB_DEV, axis=0)
    member_side = (jnp.arange(QBLOCKS, dtype=jnp.int32) % QB_DEV)[:, None]
    allowed = jnp.repeat(assigned_rows == member_side, PB_DEV, axis=1)
    noise = jax.random.randint(key_noise, (QBLOCKS, NPB), 0, 65536)
    coin = jax.random.randint(key_coin, (QBLOCKS, NPB), 0, 2)
    order = jnp.arange(NPB, dtype=jnp.int32)[None, :]
    priority = noise * NPB + order + jnp.where(hot[None, :], coin, 0) * (65536 * NPB)
    priority = priority + allowed.astype(jnp.int32) * (2 * 65536 * NPB)
    ignored, chosen = lax.top_k(priority, LMAX)
    counts = jax.random.randint(key_count, (QBLOCKS,), 6, LMAX + 1)
    counts = jnp.where(jnp.arange(QBLOCKS) == 0, LMAX, counts)
    slots = jnp.arange(LMAX, dtype=jnp.int32)[None, :]
    return jnp.where(slots < counts[:, None], chosen, -1).astype(jnp.int32)


def draw_queries(key, part):
    key = jax.random.fold_in(key, 1)
    base = jnp.clip(jax.random.normal(key, (Q, D), jnp.float32), -6.0, 6.0)
    values = base
    return jnp.clip(values, -24.0, 24.0).astype(jnp.bfloat16)


def draw_passages(key, part):
    key = jax.random.fold_in(key, 2)
    base = jnp.clip(jax.random.normal(key, (P_SIZE, D), jnp.float32), -6.0, 6.0)
    values = base
    return jnp.clip(values, -24.0, 24.0).astype(jnp.bfloat16)


def draw_lists(key, part):
    return listed_blocks(key)


def draw_positive(key, part):
    chosen = listed_blocks(key)
    key = jax.random.fold_in(key, 4)
    offset = jax.random.randint(key, (Q,), 0, PBLK)
    rows = jnp.arange(Q, dtype=jnp.int32) // QROWS
    return (chosen[rows, 0] * PBLK + offset).astype(jnp.int32)


def setup_inputs(seed: int = 0) -> dict:
    streams_of = jax.random.split(jax.random.key(seed), 5)
    queries = draw_queries(jax.random.fold_in(streams_of[4], 71), 0)
    passages = draw_passages(jax.random.fold_in(streams_of[4], 71), 0)
    lists = draw_lists(jax.random.fold_in(streams_of[4], 71), 0)
    positive = draw_positive(jax.random.fold_in(streams_of[4], 71), 0)
    return dict(queries=queries, passages=passages, lists=lists, positive=positive)


def reference(queries, passages, lists, positive):
    scale = float(D) ** -0.5
    blocks = passages.astype(jnp.float32).reshape(NPB, PBLK, D)
    query_blocks = queries.astype(jnp.float32).reshape(QBLOCKS, QROWS, D)
    positive_blocks = positive.reshape(QBLOCKS, QROWS)

    def one_block(items):
        rows, ids, wanted = items
        valid = ids >= 0
        picked = blocks[jnp.maximum(ids, 0)]
        scores = jnp.einsum("rd,lkd->rlk", rows, picked, precision=lax.Precision.HIGHEST) * scale
        masked = jnp.where(valid[None, :, None], scores, -jnp.inf)
        top = jnp.max(masked, axis=(1, 2))
        total = jnp.sum(jnp.where(valid[None, :, None], jnp.exp(scores - top[:, None, None]), 0.0), axis=(1, 2))
        global_rows = ids[:, None] * PBLK + jnp.arange(PBLK, dtype=jnp.int32)[None, :]
        hit = (global_rows[None, :, :] == wanted[:, None, None]) & valid[None, :, None]
        chosen = jnp.sum(jnp.where(hit, scores, 0.0), axis=(1, 2))
        return top + jnp.log(total) - chosen

    loss = lax.map(one_block, (query_blocks, lists, positive_blocks))
    return loss.reshape(Q)
```

```python
import functools

import jax
import jax.numpy as jnp
from jax import lax
from jax.experimental import pallas as pl
from jax.experimental.pallas import tpu as pltpu
from jax.sharding import Mesh
from jax.sharding import PartitionSpec as P

QROWS = 128
PBLK = 256
RING = 4
AXES = ("z", "core", "y", "x")
REL = (0, -1, 1, 2)


def ring(axis, step):
    return [(i, (i + step) % RING) for i in range(RING)]


def shift(array, axis, step):
    return lax.ppermute(array, axis, ring(axis, step))


def device(z, core, y, x):
    return ((z * 2 + core) * RING + y) * RING + x


def shift_zy(array, first, step):
    pairs = []
    for z in range(RING):
        for core in range(2):
            for y in range(RING):
                for x in range(RING):
                    along_z = (core == 0) == first
                    to_z = (z + step) % RING if along_z else z
                    to_y = y if along_z else (y + step) % RING
                    pairs.append((device(z, core, y, x), device(to_z, core, to_y, x)))
    return lax.ppermute(array, AXES, pairs)


def swap(array):
    return lax.ppermute(array, "core", [(0, 1), (1, 0)])


def score_kernel(parts, groups, scale, has_init, info, *refs):
    refs = list(refs)
    meta = refs.pop(0)
    init = refs.pop(0) if has_init else None
    queries = [[refs.pop(0) for _ in rows] for rows in parts]
    pieces = [[refs.pop(0) for _ in range(5)] for _ in groups]
    out, q_buf, p_buf, q_sem, p_sem = refs
    me_z, me_core, me_y, me_x = (info[k] for k in range(4))
    feats = q_buf.shape[2] // 8

    def turn(value, step):
        return lax.rem(value + step + RING, RING)

    def load_queries(s):
        for n, (ref, rows) in enumerate(zip(queries[s], parts[s])):
            start, size = rows
            pltpu.make_async_copy(ref, q_buf.at[s, pl.ds(start, size)], q_sem.at[s]).start()

    def load_slot(g, k, source):
        for m in range(RING):
            i, j = (k, m) if source == 0 else (m, k)
            ref, at = (pieces[g][i], j) if i < 3 else (pieces[g][3 + j // 2], j % 2)
            zsrc = turn(me_z, REL[m])
            for c in range(2):
                column = pl.multiple_of((zsrc * 2 + (source ^ c)) * feats, feats)
                pltpu.make_async_copy(
                    ref.at[at, c],
                    p_buf.at[g * RING + k, :, pl.ds(column, feats)],
                    p_sem.at[g * RING + k],
                ).start()

    def load_group(g, ks):
        for source in range(2):
            @pl.when((me_core + groups[g]) % 2 == source)
            def _():
                for k in ks:
                    load_slot(g, k, source)

    load_queries(0)
    load_group(0, (0,))
    for s in range(1, len(parts)):
        load_queries(s)
    load_group(0, (1, 2, 3))
    for g in range(1, len(groups)):
        load_group(g, (0, 1, 2, 3))

    if has_init:
        out[...] = init[...]
    else:
        rows = lax.broadcasted_iota(jnp.int32, out.shape, 1)
        out[...] = jnp.where(rows == 0, -1e30, 0.0).astype(jnp.float32)

    def block(k, s):
        source = lax.rem(me_core + (groups[0] if len(groups) == 1 else k // RING), 2)
        rel = lax.rem(k, RING)
        offset = jnp.where(rel == 3, 2, jnp.where(rel == 1, -1, rel // 2))
        block_id = (turn(me_y, offset) * RING + me_x) * 2 + source
        scores = lax.dot_general(
            p_buf[k], q_buf[s], (((1,), (1,)), ((), ())), preferred_element_type=jnp.float32
        ) * scale
        listed = jnp.max((meta[s, 0:8, :] == block_id).astype(jnp.int32), axis=0, keepdims=True) > 0
        wanted = meta[s, 8:9, :] - block_id * PBLK
        top, total, chosen = out[s, 0:1, :], out[s, 1:2, :], out[s, 2:3, :]
        new_top = jnp.where(listed, jnp.maximum(top, jnp.max(scores, axis=0, keepdims=True)), top)
        here = jnp.sum(jnp.exp(scores - new_top), axis=0, keepdims=True)
        index = lax.broadcasted_iota(jnp.int32, scores.shape, 0)
        hit = jnp.sum(jnp.where(index == wanted, scores, 0.0), axis=0, keepdims=True)
        out[s, 0:1, :] = new_top
        out[s, 1:2, :] = total * jnp.exp(top - new_top) + jnp.where(listed, here, 0.0)
        out[s, 2:3, :] = chosen + hit

    def whole(ref, sem):
        pltpu.make_async_copy(ref, ref, sem).wait()

    @pl.loop(0, len(groups) * RING)
    def _(k):
        whole(p_buf.at[k], p_sem.at[k])

        @pl.loop(0, len(parts))
        def _(s):
            @pl.when(k == 0)
            def _():
                whole(q_buf.at[s], q_sem.at[s])

            block(k, s)


def score(info, meta, queries, pieces, groups, init=None):
    features = queries[0][0].shape[1]
    parts = []
    for arrays in queries:
        start, rows = 0, []
        for a in arrays:
            rows.append((start, a.shape[0]))
            start += a.shape[0]
        parts.append(tuple(rows))
    count, blocks = len(parts), len(groups) * RING
    size = 2 * QROWS
    flat = [a for arrays in queries for a in arrays] + [a for arrays in pieces for a in arrays]
    vmem = pl.BlockSpec(memory_space=pltpu.VMEM)
    shape = (count, 3, size)
    head = [meta] + ([init] if init is not None else [])
    kernel = functools.partial(
        score_kernel, tuple(parts), groups, float(features) ** -0.5, init is not None
    )
    return pl.pallas_call(
        kernel,
        out_shape=jax.ShapeDtypeStruct(shape, jnp.float32),
        in_specs=[pl.BlockSpec(memory_space=pltpu.SMEM)]
        + [vmem] * len(head)
        + [pl.BlockSpec(memory_space=pl.ANY)] * len(flat),
        out_specs=vmem,
        scratch_shapes=[
            pltpu.VMEM((count, size, features), jnp.bfloat16),
            pltpu.VMEM((blocks, PBLK, features), jnp.bfloat16),
            pltpu.SemaphoreType.DMA((count,)),
            pltpu.SemaphoreType.DMA((blocks,)),
        ],
        compiler_params=pltpu.CompilerParams(vmem_limit_bytes=32 * 1024 * 1024),
        cost_estimate=pl.CostEstimate(
            flops=2 * count * size * blocks * PBLK * features,
            bytes_accessed=(count * size + blocks * PBLK) * features * 2,
            transcendentals=count * size * blocks * PBLK,
        ),
    )(info, *head, *flat)


def finish(stats):
    top, total, chosen = stats[:, 0], stats[:, 1], stats[:, 2]
    peak = jnp.max(top, axis=0)
    summed = jnp.sum(total * jnp.exp(top - peak[None, :]), axis=0)
    return peak + jnp.log(summed) - jnp.sum(chosen, axis=0)


def body(queries, passages, lists, positive):
    info = jnp.stack([lax.axis_index(a) for a in AXES]).astype(jnp.int32)
    core = lax.axis_index("core")
    half = QROWS

    meta = jnp.concatenate([jnp.repeat(lists.T, QROWS, axis=1), positive[None, :]], axis=0)
    top, bottom = queries[:half], queries[half:]
    r0, l1 = shift(top, "x", 1), shift(bottom, "x", -1)
    r1, l0 = shift(bottom, "x", 1), shift(top, "x", -1)
    f0, f1 = shift(r0, "x", 1), shift(l1, "x", -1)
    meta_r, meta_l, meta_f = shift(meta, "x", 1), shift(meta, "x", -1), shift(meta, "x", 2)

    blocks = passages.reshape(2, PBLK, passages.shape[1])
    mine = lax.dynamic_index_in_dim(blocks, core, 0, keepdims=False)
    other = lax.dynamic_index_in_dim(blocks, 1 - core, 0, keepdims=False)
    piece = jnp.stack([mine, swap(other)])
    s = jnp.stack(
        [piece, shift_zy(piece, True, 1), shift_zy(piece, True, -1), shift_zy(piece, True, 2)]
    )
    pr, pl_ = shift_zy(s, False, 1), shift_zy(s, False, -1)
    fr, fl = shift_zy(pr[:2], False, 1), shift_zy(pl_[2:], False, -1)
    own = [s, pr, pl_, fr, fl]
    theirs = [swap(a) for a in own]

    near = [[queries], [r0, r1], [l0, l1]]
    metas = jnp.stack([meta, meta_r, meta_l])
    stats = score(info, metas, near, [own], (0,))
    stats = score(info, metas, near, [theirs], (1,), stats)
    far = score(info, meta_f[None], [[f0, f1]], [own, theirs], (0, 1))
    back = [
        stats[0],
        shift(stats[1], "x", -1),
        shift(stats[2], "x", 1),
        shift(far[0], "x", 2),
    ]
    return finish(jnp.stack(back))


def solution(mesh):
    fine = Mesh(mesh.devices.reshape(RING, 2, RING, RING), AXES)
    everywhere = ("z", "core", "y", "x")
    return jax.shard_map(
        body,
        mesh=fine,
        in_specs=(
            P(everywhere, None),
            P(("y", "x"), ("z", "core")),
            P(everywhere, None),
            P(everywhere),
        ),
        out_specs=P(everywhere),
        check_vma=False,
    )
```

```python
import functools

import jax
import jax.numpy as jnp
from jax import lax
from jax.experimental import pallas as pl
from jax.experimental.pallas import tpu as pltpu
from jax.sharding import Mesh
from jax.sharding import PartitionSpec as P

QROWS = 128
PBLK = 256
LISTED = 8
PIECES = 8
RING = 4
PACE_M, PACE_A, PACE_B = 4, 10, 5
AXES = ("z", "core", "y", "x")
VMEM = 60 * 1024 * 1024
REL = (0, -1, 1, 2)


def ring(axis, step):
    return [(i, (i + step) % RING) for i in range(RING)]


def shift(array, axis, step):
    return lax.ppermute(array, axis, ring(axis, step))


def device(z, core, y, x):
    return ((z * 2 + core) * RING + y) * RING + x


def shift_zy(array, first, step):
    pairs = []
    for z in range(RING):
        for core in range(2):
            for y in range(RING):
                for x in range(RING):
                    along_z = (core == 0) == first
                    to_z = (z + step) % RING if along_z else z
                    to_y = y if along_z else (y + step) % RING
                    pairs.append((device(z, core, y, x), device(to_z, core, to_y, x)))
    return lax.ppermute(array, AXES, pairs)


def shift_x(array, step):
    pairs = []
    for core in range(2):
        for x in range(RING):
            pairs.append((core * RING + x, core * RING + (x + (1 - 2 * core) * step) % RING))
    return lax.ppermute(array, ("core", "x"), pairs)


def both(array):
    return array, swap(array)


def swap(array):
    return lax.ppermute(array, "core", [(0, 1), (1, 0)])


def token(arrays, us):
    def kernel(*refs):
        refs[-1][...] = jnp.zeros_like(refs[-1])

    return pl.pallas_call(
        kernel,
        out_shape=jax.ShapeDtypeStruct((8, 128), jnp.float32),
        in_specs=[pl.BlockSpec(memory_space=pl.ANY)] * len(arrays),
        out_specs=pl.BlockSpec(memory_space=pltpu.VMEM),
        compiler_params=pltpu.CompilerParams(vmem_limit_bytes=VMEM),
        cost_estimate=pl.CostEstimate(
            flops=int(us * 1.15e9), bytes_accessed=0, transcendentals=0
        ),
    )(*arrays)


def after(array, tokens):
    def kernel(*refs):
        pass

    anywhere = pl.BlockSpec(memory_space=pl.ANY)
    return pl.pallas_call(
        kernel,
        out_shape=jax.ShapeDtypeStruct(array.shape, array.dtype),
        in_specs=[anywhere] * (1 + len(tokens)),
        out_specs=anywhere,
        input_output_aliases={0: 0},
        compiler_params=pltpu.CompilerParams(vmem_limit_bytes=VMEM),
        cost_estimate=pl.CostEstimate(flops=1000, bytes_accessed=0, transcendentals=0),
    )(array, *tokens)


def score_kernel(first, extra, scale, info, lists, positive, *refs):
    refs = list(refs)
    queries = [refs.pop(0) for _ in range(2)]
    pieces = [[refs.pop(0) for _ in range(PIECES)] for _ in range(2)] if first else refs.pop(0)
    del refs[:extra]
    outs = [refs.pop(0) for _ in range(2)]
    whole = refs.pop(0) if first else None
    q_all, p_buf, a_sem, p_sem, w_sem = refs
    me_z, me_core, me_y, me_x = (info[k] for k in range(4))
    feats = p_buf.shape[2] // 8

    def turn(value, step):
        return lax.rem(value + step + RING, RING)

    def any_of(s, block, test):
        found = test(lists[s, block * LISTED])
        for n in range(1, LISTED):
            found = jnp.logical_or(found, test(lists[s, block * LISTED + n]))
        return found

    def load_passages(k, source):
        g = lax.rem(me_core + source, 2)
        for which in range(2):
            @pl.when(g == which)
            def _():
                for m in range(RING):
                    i, j = (k, m) if source == 0 else (m, k)
                    column = pl.multiple_of((turn(me_z, REL[m]) * 2 + source) * feats, feats)
                    pltpu.make_async_copy(
                        pieces[which][i * 2 + j // 2].at[j % 2],
                        p_buf.at[k, :, pl.ds(column, feats)],
                        p_sem.at[k],
                    ).start()

    def load_whole(k):
        pltpu.make_async_copy(pieces.at[k], p_buf.at[k], p_sem.at[k]).start()

    for s in range(2):
        pltpu.make_async_copy(queries[s], q_all.at[s], a_sem.at[s]).start()
    for k in range(RING):
        if first:
            for source in range(2):
                load_passages(k, source)
        elif k < 2:
            load_whole(k)

    def owner_of(k):
        return turn(me_y, jnp.where(k == 3, 2, jnp.where(k == 2, 1, -k))) * RING + me_x

    def choose(k, s):
        owner = owner_of(k)
        block = any_of(s, 1, lambda b: lax.shift_right_arithmetic(b, 1) == owner)
        block = block.astype(jnp.int32)
        return block, pl.ds(pl.multiple_of(block * QROWS, QROWS), QROWS)

    for out in outs:
        rows = lax.broadcasted_iota(jnp.int32, out.shape, 0)
        out[...] = jnp.where(rows == 0, -1e30, 0.0).astype(jnp.float32)
    for s in range(2):
        pltpu.make_async_copy(q_all.at[s], q_all.at[s], a_sem.at[s]).wait()

    @pl.loop(0, RING)
    def _(k):
        index = lax.broadcasted_iota(jnp.int32, (PBLK, 2 * QROWS), 0)
        left = lax.broadcasted_iota(jnp.int32, (1, 2 * QROWS), 1) < QROWS
        owner = owner_of(k)
        chosen, lanes = zip(*[choose(k, s) for s in range(2)])
        listed = []
        for b in range(2):
            sides = [
                any_of(s, chosen[s], lambda v: v == owner * 2 + b).astype(jnp.int32)
                for s in range(2)
            ]
            listed.append(jnp.where(left, sides[0], sides[1]) > 0)
        pltpu.make_async_copy(p_buf.at[k], p_buf.at[k], p_sem.at[k]).wait()
        if first:
            pltpu.make_async_copy(p_buf.at[k], whole.at[k], w_sem.at[k]).start()
        else:
            @pl.when(k + 2 < RING)
            def _():
                load_whole(k + 2)
        rows = jnp.concatenate([q_all[s, lanes[s], :] for s in range(2)], axis=0)
        scores = lax.dot_general(
            p_buf[k], rows, (((1,), (1,)), ((), ())), preferred_element_type=jnp.float32
        ) * scale

        def get(row):
            return jnp.concatenate([outs[s][row : row + 1, lanes[s]] for s in range(2)], axis=1)

        wanted = jnp.concatenate([positive[s : s + 1, lanes[s]] for s in range(2)], axis=1)
        old = get(0)
        halves = [scores[:PBLK], scores[PBLK:]]
        top = old
        for b in range(2):
            peak = jnp.max(halves[b], axis=0, keepdims=True)
            top = jnp.where(listed[b], jnp.maximum(top, peak), top)
        total = get(1) * jnp.exp(old - top)
        hits = get(2)
        for b in range(2):
            here = jnp.sum(jnp.exp(halves[b] - top), axis=0, keepdims=True)
            total = total + jnp.where(listed[b], here, 0.0)
            place = wanted - (owner * 2 + b) * PBLK
            hits = hits + jnp.sum(jnp.where(index == place, halves[b], 0.0), axis=0, keepdims=True)
        for s in range(2):
            part = slice(s * QROWS, (s + 1) * QROWS)
            outs[s][0:1, lanes[s]] = top[:, part]
            outs[s][1:2, lanes[s]] = total[:, part]
            outs[s][2:3, lanes[s]] = hits[:, part]

    if first:
        for k in range(RING):
            pltpu.make_async_copy(p_buf.at[k], whole.at[k], w_sem.at[k]).wait()


def score(info, lists, positive, queries, pieces, extra=()):
    first = isinstance(pieces, list)
    rows, features = queries[0].shape
    flat = list(queries) + ([a for arrays in pieces for a in arrays] if first else [pieces])
    flat += list(extra)
    smem, vmem = pl.BlockSpec(memory_space=pltpu.SMEM), pl.BlockSpec(memory_space=pltpu.VMEM)
    anywhere = pl.BlockSpec(memory_space=pl.ANY)
    stats = [jax.ShapeDtypeStruct((3, rows), jnp.float32)] * 2
    whole = jax.ShapeDtypeStruct((RING, 2 * PBLK, features), jnp.bfloat16)
    return pl.pallas_call(
        functools.partial(score_kernel, first, len(extra), float(features) ** -0.5),
        out_shape=stats + [whole] * first,
        in_specs=[smem, smem, vmem] + [anywhere] * len(flat),
        out_specs=[vmem, vmem] + [anywhere] * first,
        scratch_shapes=[
            pltpu.VMEM((2, rows, features), jnp.bfloat16),
            pltpu.VMEM((RING, 2 * PBLK, features), jnp.bfloat16),
            pltpu.SemaphoreType.DMA((2,)),
            pltpu.SemaphoreType.DMA((RING,)),
            pltpu.SemaphoreType.DMA((RING,)),
        ],
        compiler_params=pltpu.CompilerParams(vmem_limit_bytes=VMEM),
        cost_estimate=pl.CostEstimate(flops=1000000, bytes_accessed=0, transcendentals=0),
    )(info, lists, positive, *flat)


def finish(stats):
    top, total, chosen = stats[:, 0], stats[:, 1], stats[:, 2]
    peak = jnp.max(top, axis=0)
    summed = jnp.sum(total * jnp.exp(top - peak[None, :]), axis=0)
    return peak + jnp.log(summed) - jnp.sum(chosen, axis=0)


def body(queries, passages, lists, positive):
    info = jnp.stack([lax.axis_index(a) for a in AXES]).astype(jnp.int32)

    meta = jnp.concatenate([positive, lists.reshape(-1)])
    ahead, behind = shift_x(queries, 1), shift_x(queries, -1)
    far = shift_x(ahead, 1)
    meta_a, meta_b, meta_f = shift_x(meta, 1), shift_x(meta, -1), shift_x(meta, 2)

    s01 = jnp.stack([passages, shift_zy(passages, True, 1)])
    s23 = jnp.stack([shift_zy(passages, True, -1), shift_zy(passages, True, 2)])
    r01, l01 = shift_zy(s01, False, 1), shift_zy(s01, False, -1)
    l23, r23 = shift_zy(s23, False, -1), shift_zy(s23, False, 1)
    gate = token([ahead, token([meta_a, meta_b, meta_f], PACE_M)], PACE_A)
    fr = shift_zy(after(r01, [gate]), False, 1)
    fl = shift_zy(l23, False, -1)
    gate = token([behind], PACE_B)
    fr, fl = after(fr, [gate]), after(fl, [gate])
    pieces = [both(a) for a in (s01, s23, r01, r23, l01, l23, fr, fl)]
    pieces = [[a for a, _ in pieces], [b for _, b in pieces]]

    size = positive.shape[0]

    def pair(metas, sources, passages, extra=()):
        wanted = jnp.stack([m[:size] for m in metas])
        ids = jnp.stack([m[size:] for m in metas])
        return score(info, ids, wanted, sources, passages, extra)

    stats_a, stats_b, whole = pair([meta_a, meta_b], [ahead, behind], pieces)
    back = [shift_x(stats_a, -1), shift_x(stats_b, 1)]
    stats_o, stats_f = pair([meta, meta_f], [queries, far], whole, back)
    return finish(jnp.stack(back + [stats_o, shift_x(stats_f, 2)]))


def solution(mesh):
    fine = Mesh(mesh.devices.reshape(RING, 2, RING, RING), AXES)
    everywhere = ("z", "core", "y", "x")
    return jax.shard_map(
        body,
        mesh=fine,
        in_specs=(
            P(everywhere, None),
            P(("y", "x"), ("z", "core")),
            P(everywhere, None),
            P(everywhere),
        ),
        out_specs=P(everywhere),
        check_vma=False,
    )
```

```python
import functools

import jax
import jax.numpy as jnp
from jax import lax
from jax.experimental import pallas as pl
from jax.experimental.pallas import tpu as pltpu
from jax.sharding import Mesh
from jax.sharding import PartitionSpec as P

QROWS = 128
PBLK = 256
LISTED = 8
SOURCES = 4
PIECES = 5
RING = 4
PACE_F = 2
PACE_M, PACE_A, PACE_B = 3, 2, 8
AXES = ("z", "core", "y", "x")
VMEM = 60 * 1024 * 1024
REL = (0, -1, 1, 2)


def ring(axis, step):
    return [(i, (i + step) % RING) for i in range(RING)]


def shift(array, axis, step):
    return lax.ppermute(array, axis, ring(axis, step))


def device(z, core, y, x):
    return ((z * 2 + core) * RING + y) * RING + x


def shift_zy(array, first, step):
    pairs = []
    for z in range(RING):
        for core in range(2):
            for y in range(RING):
                for x in range(RING):
                    along_z = (core == 0) == first
                    to_z = (z + step) % RING if along_z else z
                    to_y = y if along_z else (y + step) % RING
                    pairs.append((device(z, core, y, x), device(to_z, core, to_y, x)))
    return lax.ppermute(array, AXES, pairs)


def shift_x(array, step):
    pairs = []
    for core in range(2):
        for x in range(RING):
            pairs.append((core * RING + x, core * RING + (x + (1 - 2 * core) * step) % RING))
    return lax.ppermute(array, ("core", "x"), pairs)


def both(array):
    return array, swap(array)


def swap(array):
    return lax.ppermute(array, "core", [(0, 1), (1, 0)])


def token(arrays, us):
    def kernel(*refs):
        refs[-1][...] = jnp.zeros_like(refs[-1])

    return pl.pallas_call(
        kernel,
        out_shape=jax.ShapeDtypeStruct((8, 128), jnp.float32),
        in_specs=[pl.BlockSpec(memory_space=pl.ANY)] * len(arrays),
        out_specs=pl.BlockSpec(memory_space=pltpu.VMEM),
        compiler_params=pltpu.CompilerParams(vmem_limit_bytes=VMEM),
        cost_estimate=pl.CostEstimate(
            flops=int(us * 1.15e9), bytes_accessed=0, transcendentals=0
        ),
    )(*arrays)


def after(array, tokens):
    def kernel(*refs):
        pass

    anywhere = pl.BlockSpec(memory_space=pl.ANY)
    return pl.pallas_call(
        kernel,
        out_shape=jax.ShapeDtypeStruct(array.shape, array.dtype),
        in_specs=[anywhere] * (1 + len(tokens)),
        out_specs=anywhere,
        input_output_aliases={0: 0},
        compiler_params=pltpu.CompilerParams(vmem_limit_bytes=VMEM),
        cost_estimate=pl.CostEstimate(flops=1000, bytes_accessed=0, transcendentals=0),
    )(array, *tokens)


def take(array, start, tokens):
    def kernel(ref, *refs):
        out, buf, sems = refs[-3:]
        loads, stores = [], []
        for n in range(2):
            loads.append(pltpu.make_async_copy(ref.at[start + n], buf.at[n], sems.at[n]))
            stores.append(pltpu.make_async_copy(buf.at[n], out.at[n], sems.at[2 + n]))
            loads[n].start()
        for n in range(2):
            loads[n].wait()
            stores[n].start()
        for n in range(2):
            stores[n].wait()

    anywhere = pl.BlockSpec(memory_space=pl.ANY)
    return pl.pallas_call(
        kernel,
        out_shape=jax.ShapeDtypeStruct((2, *array.shape[1:]), array.dtype),
        in_specs=[anywhere] * (1 + len(tokens)),
        out_specs=anywhere,
        scratch_shapes=[pltpu.VMEM((2, *array.shape[1:]), array.dtype), pltpu.SemaphoreType.DMA((4,))],
        compiler_params=pltpu.CompilerParams(vmem_limit_bytes=VMEM),
        cost_estimate=pl.CostEstimate(flops=1000, bytes_accessed=0, transcendentals=0),
    )(array, *tokens)


def score_kernel(extra, scale, info, lists, positive, *refs):
    refs = list(refs)
    queries = [refs.pop(0) for _ in range(SOURCES)]
    pieces = [[refs.pop(0) for _ in range(PIECES)] for _ in range(2)]
    del refs[:extra]
    outs, q_all, p_buf, a_sem, p_sem = refs
    me_z, me_core, me_y, me_x = (info[k] for k in range(4))
    feats = p_buf.shape[2] // 8

    def turn(value, step):
        return lax.rem(value + step + RING, RING)

    def any_of(s, block, test):
        found = test(lists[s, block * LISTED])
        for n in range(1, LISTED):
            found = jnp.logical_or(found, test(lists[s, block * LISTED + n]))
        return found

    def load_passages(k, source):
        g = lax.rem(me_core + source, 2)
        for which in range(2):
            @pl.when(g == which)
            def _():
                for m in range(RING):
                    i, j = (k, m) if source == 0 else (m, k)
                    column = pl.multiple_of((turn(me_z, REL[m]) * 2 + source) * feats, feats)
                    n, at = (i, j) if i < 3 else (3 + j // 2, j % 2)
                    pltpu.make_async_copy(
                        pieces[which][n].at[at], p_buf.at[k, :, pl.ds(column, feats)], p_sem.at[k]
                    ).start()

    def load_slot(k):
        for source in range(2):
            load_passages(k, source)

    def load_pair(pair):
        for s in pair:
            pltpu.make_async_copy(queries[s], q_all.at[s], a_sem.at[s]).start()

    load_slot(0)
    load_pair((0, 1))
    load_pair((2, 3))
    load_slot(1)

    def owner_of(k):
        return turn(me_y, jnp.where(k == 3, 2, jnp.where(k == 2, 1, -k))) * RING + me_x

    def choose(k, s):
        owner = owner_of(k)
        block = any_of(s, 1, lambda b: lax.shift_right_arithmetic(b, 1) == owner)
        block = block.astype(jnp.int32)
        return block, pl.ds(pl.multiple_of(block * QROWS, QROWS), QROWS)

    rows = lax.broadcasted_iota(jnp.int32, outs.shape, 1)
    outs[...] = jnp.where(rows == 0, -1e30, 0.0).astype(jnp.float32)
    def multiply(k, pair):
        index = lax.broadcasted_iota(jnp.int32, (PBLK, 2 * QROWS), 0)
        left = lax.broadcasted_iota(jnp.int32, (1, 2 * QROWS), 1) < QROWS
        owner = owner_of(k)
        chosen, lanes = zip(*[choose(k, s) for s in pair])
        listed = []
        for b in range(2):
            sides = [
                any_of(s, block, lambda v: v == owner * 2 + b).astype(jnp.int32)
                for s, block in zip(pair, chosen)
            ]
            listed.append(jnp.where(left, sides[0], sides[1]) > 0)
        rows = jnp.concatenate([q_all[s, part, :] for s, part in zip(pair, lanes)], axis=0)
        scores = lax.dot_general(
            p_buf[k], rows, (((1,), (1,)), ((), ())), preferred_element_type=jnp.float32
        ) * scale

        def get(row):
            found = [outs[s, row : row + 1, part] for s, part in zip(pair, lanes)]
            return jnp.concatenate(found, axis=1)

        wanted = jnp.concatenate(
            [positive[s, :, part] for s, part in zip(pair, lanes)], axis=1
        )
        old = get(0)
        halves = [scores[:PBLK], scores[PBLK:]]
        top = old
        for b in range(2):
            peak = jnp.max(halves[b], axis=0, keepdims=True)
            top = jnp.where(listed[b], jnp.maximum(top, peak), top)
        total = get(1) * jnp.exp(old - top)
        hits = get(2)
        for b in range(2):
            here = jnp.sum(jnp.exp(halves[b] - top), axis=0, keepdims=True)
            total = total + jnp.where(listed[b], here, 0.0)
            place = wanted - (owner * 2 + b) * PBLK
            hits = hits + jnp.sum(jnp.where(index == place, halves[b], 0.0), axis=0, keepdims=True)
        for n, (s, part) in enumerate(zip(pair, lanes)):
            side = slice(n * QROWS, (n + 1) * QROWS)
            outs[s, 0:1, part] = top[:, side]
            outs[s, 1:2, part] = total[:, side]
            outs[s, 2:3, part] = hits[:, side]

    @pl.loop(0, 2 * RING)
    def _(step):
        k, second = step // 2, lax.rem(step, 2)
        pair = (second * 2, second * 2 + 1)

        @pl.when(second == 0)
        def _():
            pltpu.make_async_copy(p_buf.at[k], p_buf.at[k], p_sem.at[k]).wait()
            for later in range(2, RING):
                @pl.when(k + 2 == later)
                def _():
                    load_slot(later)

        @pl.when(k == 0)
        def _():
            for s in pair:
                pltpu.make_async_copy(q_all.at[s], q_all.at[s], a_sem.at[s]).wait()

        multiply(k, pair)


def score(info, lists, positive, queries, pieces, extra=()):
    rows, features = queries[0].shape
    flat = list(queries) + [a for arrays in pieces for a in arrays]
    flat += list(extra)
    smem, vmem = pl.BlockSpec(memory_space=pltpu.SMEM), pl.BlockSpec(memory_space=pltpu.VMEM)
    anywhere = pl.BlockSpec(memory_space=pl.ANY)
    stats = jax.ShapeDtypeStruct((SOURCES, 3, rows), jnp.float32)
    return pl.pallas_call(
        functools.partial(score_kernel, len(extra), float(features) ** -0.5),
        out_shape=stats,
        in_specs=[smem, smem, vmem] + [anywhere] * len(flat),
        out_specs=vmem,
        scratch_shapes=[
            pltpu.VMEM((SOURCES, rows, features), jnp.bfloat16),
            pltpu.VMEM((RING, 2 * PBLK, features), jnp.bfloat16),
            pltpu.SemaphoreType.DMA((SOURCES,)),
            pltpu.SemaphoreType.DMA((RING,)),
        ],
        compiler_params=pltpu.CompilerParams(vmem_limit_bytes=VMEM),
        cost_estimate=pl.CostEstimate(flops=1000000, bytes_accessed=0, transcendentals=0),
    )(info, lists, positive, *flat)


def finish(stats):
    top, total, chosen = stats[:, 0], stats[:, 1], stats[:, 2]
    peak = jnp.max(top, axis=0)
    summed = jnp.sum(total * jnp.exp(top - peak[None, :]), axis=0)
    return peak + jnp.log(summed) - jnp.sum(chosen, axis=0)


def body(queries, passages, lists, positive):
    info = jnp.stack([lax.axis_index(a) for a in AXES]).astype(jnp.int32)

    size, slots = positive.shape[0], lists.size
    meta = jnp.pad(positive, (0, slots)) + jnp.pad(lists.reshape(-1), (size, 0))
    ahead, behind = shift_x(queries, 1), shift_x(queries, -1)
    ahead = after(ahead, [token([behind], PACE_B)])
    far = shift_x(ahead, 1)
    meta_a = shift_x(meta, 1)
    meta_f = shift_x(meta_a, 1)
    meta_b = shift_x(meta_f, 1)

    s = jnp.stack([passages] + [shift_zy(passages, True, step) for step in (1, -1, 2)])
    s = after(s, [token([meta_b, meta_f, meta_a], PACE_M)])
    pr, pl_ = shift_zy(s, False, 1), shift_zy(s, False, -1)
    sides = [both(s)]
    gate = token([sides[0][1]], PACE_A)
    fr = shift_zy(take(pr, 0, [gate]), False, 1)
    fl = shift_zy(take(pl_, 2, [gate]), False, -1)
    sides += [both(a) for a in (pr, pl_, fr, fl)]
    pieces = [[a for a, _ in sides], [b for _, b in sides]]

    metas = [meta, meta_a, meta_b, meta_f]
    wanted = jnp.stack([m[None, :size] for m in metas])
    ids = jnp.stack([m[size:] for m in metas])
    info = after(info, [token([far], PACE_F)])
    stats = score(info, ids, wanted, [queries, ahead, behind, far], pieces)
    back = [shift_x(a, step) for a, step in zip(stats[1:], (-1, 1, 2))]
    return finish(jnp.stack([stats[0]] + back))


def solution(mesh):
    fine = Mesh(mesh.devices.reshape(RING, 2, RING, RING), AXES)
    everywhere = ("z", "core", "y", "x")
    return jax.shard_map(
        body,
        mesh=fine,
        in_specs=(
            P(everywhere, None),
            P(("y", "x"), ("z", "core")),
            P(everywhere, None),
            P(everywhere),
        ),
        out_specs=P(everywhere),
        check_vma=False,
    )
```

```python
import functools

import jax
import jax.numpy as jnp
from jax import lax
from jax.experimental import pallas as pl
from jax.experimental.pallas import tpu as pltpu
from jax.sharding import Mesh
from jax.sharding import PartitionSpec as P

QROWS = 128
PBLK = 256
LISTED = 8
SOURCES = 4
PIECES = 5
RING = 4
PACE_F = 2
PACE_M, PACE_A, PACE_B = 3, 5, 8
AXES = ("z", "core", "y", "x")
VMEM = 60 * 1024 * 1024
REL = (0, -1, 1, 2)


def ring(axis, step):
    return [(i, (i + step) % RING) for i in range(RING)]


def shift(array, axis, step):
    return lax.ppermute(array, axis, ring(axis, step))


def device(z, core, y, x):
    return ((z * 2 + core) * RING + y) * RING + x


def shift_zy(array, first, step):
    pairs = []
    for z in range(RING):
        for core in range(2):
            for y in range(RING):
                for x in range(RING):
                    along_z = (core == 0) == first
                    to_z = (z + step) % RING if along_z else z
                    to_y = y if along_z else (y + step) % RING
                    pairs.append((device(z, core, y, x), device(to_z, core, to_y, x)))
    return lax.ppermute(array, AXES, pairs)


def shift_x(array, step):
    pairs = []
    for core in range(2):
        for x in range(RING):
            pairs.append((core * RING + x, core * RING + (x + (1 - 2 * core) * step) % RING))
    return lax.ppermute(array, ("core", "x"), pairs)


def both(array):
    return array, swap(array)


def swap(array):
    return lax.ppermute(array, "core", [(0, 1), (1, 0)])


def token(arrays, us):
    def kernel(*refs):
        refs[-1][...] = jnp.zeros_like(refs[-1])

    return pl.pallas_call(
        kernel,
        out_shape=jax.ShapeDtypeStruct((8, 128), jnp.float32),
        in_specs=[pl.BlockSpec(memory_space=pl.ANY)] * len(arrays),
        out_specs=pl.BlockSpec(memory_space=pltpu.VMEM),
        compiler_params=pltpu.CompilerParams(vmem_limit_bytes=VMEM),
        cost_estimate=pl.CostEstimate(
            flops=int(us * 1.15e9), bytes_accessed=0, transcendentals=0
        ),
    )(*arrays)


def after(array, tokens):
    def kernel(*refs):
        pass

    anywhere = pl.BlockSpec(memory_space=pl.ANY)
    return pl.pallas_call(
        kernel,
        out_shape=jax.ShapeDtypeStruct(array.shape, array.dtype),
        in_specs=[anywhere] * (1 + len(tokens)),
        out_specs=anywhere,
        input_output_aliases={0: 0},
        compiler_params=pltpu.CompilerParams(vmem_limit_bytes=VMEM),
        cost_estimate=pl.CostEstimate(flops=1000, bytes_accessed=0, transcendentals=0),
    )(array, *tokens)


def take(array, start, tokens):
    def kernel(ref, *refs):
        out, buf, sems = refs[-3:]
        loads, stores = [], []
        for n in range(2):
            loads.append(pltpu.make_async_copy(ref.at[start + n], buf.at[n], sems.at[n]))
            stores.append(pltpu.make_async_copy(buf.at[n], out.at[n], sems.at[2 + n]))
            loads[n].start()
        for n in range(2):
            loads[n].wait()
            stores[n].start()
        for n in range(2):
            stores[n].wait()

    anywhere = pl.BlockSpec(memory_space=pl.ANY)
    return pl.pallas_call(
        kernel,
        out_shape=jax.ShapeDtypeStruct((2, *array.shape[1:]), array.dtype),
        in_specs=[anywhere] * (1 + len(tokens)),
        out_specs=anywhere,
        scratch_shapes=[pltpu.VMEM((2, *array.shape[1:]), array.dtype), pltpu.SemaphoreType.DMA((4,))],
        compiler_params=pltpu.CompilerParams(vmem_limit_bytes=VMEM),
        cost_estimate=pl.CostEstimate(flops=1000, bytes_accessed=0, transcendentals=0),
    )(array, *tokens)


def score_kernel(extra, scale, info, lists, positive, *refs):
    refs = list(refs)
    queries = [refs.pop(0) for _ in range(SOURCES)]
    pieces = [[refs.pop(0) for _ in range(PIECES)] for _ in range(2)]
    del refs[:extra]
    results = [refs.pop(0) for _ in range(SOURCES)]
    outs, q_all, p_buf, a_sem, p_sem = refs
    me_z, me_core, me_y, me_x = (info[k] for k in range(4))
    feats = p_buf.shape[2] // 8

    def turn(value, step):
        return lax.rem(value + step + RING, RING)

    def any_of(s, block, test):
        found = test(lists[s, block * LISTED])
        for n in range(1, LISTED):
            found = jnp.logical_or(found, test(lists[s, block * LISTED + n]))
        return found

    def load_passages(k, source):
        g = lax.rem(me_core + source, 2)
        for which in range(2):
            @pl.when(g == which)
            def _():
                for m in range(RING):
                    i, j = (k, m) if source == 0 else (m, k)
                    column = pl.multiple_of((turn(me_z, REL[m]) * 2 + source) * feats, feats)
                    n, at = (i, j) if i < 3 else (3 + j // 2, j % 2)
                    pltpu.make_async_copy(
                        pieces[which][n].at[at], p_buf.at[k, :, pl.ds(column, feats)], p_sem.at[k]
                    ).start()

    def load_slot(k):
        for source in range(2):
            load_passages(k, source)

    def load_pair(pair):
        for s in pair:
            pltpu.make_async_copy(queries[s], q_all.at[s], a_sem.at[s]).start()

    load_slot(0)
    load_pair((0, 1))

    def owner_of(k):
        return turn(me_y, jnp.where(k == 3, 2, jnp.where(k == 2, 1, -k))) * RING + me_x

    def choose(k, s):
        owner = owner_of(k)
        block = any_of(s, 1, lambda b: lax.shift_right_arithmetic(b, 1) == owner)
        block = block.astype(jnp.int32)
        return block, pl.ds(pl.multiple_of(block * QROWS, QROWS), QROWS)

    rows = lax.broadcasted_iota(jnp.int32, outs.shape, 1)
    outs[...] = jnp.where(rows == 0, -1e30, 0.0).astype(jnp.float32)
    def multiply(k, pair):
        index = lax.broadcasted_iota(jnp.int32, (PBLK, 2 * QROWS), 0)
        left = lax.broadcasted_iota(jnp.int32, (1, 2 * QROWS), 1) < QROWS
        owner = owner_of(k)
        chosen, lanes = zip(*[choose(k, s) for s in pair])
        listed = []
        for b in range(2):
            sides = [
                any_of(s, block, lambda v: v == owner * 2 + b).astype(jnp.int32)
                for s, block in zip(pair, chosen)
            ]
            listed.append(jnp.where(left, sides[0], sides[1]) > 0)
        rows = jnp.concatenate([q_all[s, part, :] for s, part in zip(pair, lanes)], axis=0)
        scores = lax.dot_general(
            p_buf[k], rows, (((1,), (1,)), ((), ())), preferred_element_type=jnp.float32
        ) * scale

        def get(row):
            found = [outs[s, row : row + 1, part] for s, part in zip(pair, lanes)]
            return jnp.concatenate(found, axis=1)

        wanted = jnp.concatenate(
            [positive[s, :, part] for s, part in zip(pair, lanes)], axis=1
        )
        old = get(0)
        halves = [scores[:PBLK], scores[PBLK:]]
        top = old
        for b in range(2):
            peak = jnp.max(halves[b], axis=0, keepdims=True)
            top = jnp.where(listed[b], jnp.maximum(top, peak), top)
        total = get(1) * jnp.exp(old - top)
        hits = get(2)
        for b in range(2):
            here = jnp.sum(jnp.exp(halves[b] - top), axis=0, keepdims=True)
            total = total + jnp.where(listed[b], here, 0.0)
            place = wanted - (owner * 2 + b) * PBLK
            hits = hits + jnp.sum(jnp.where(index == place, halves[b], 0.0), axis=0, keepdims=True)
        for n, (s, part) in enumerate(zip(pair, lanes)):
            side = slice(n * QROWS, (n + 1) * QROWS)
            outs[s, 0:1, part] = top[:, side]
            outs[s, 1:2, part] = total[:, side]
            outs[s, 2:3, part] = hits[:, side]

    @pl.loop(0, 2 * RING)
    def _(step):
        k, second = step // 2, lax.rem(step, 2)
        pair = (second * 2, second * 2 + 1)

        @pl.when(second == 0)
        def _():
            pltpu.make_async_copy(p_buf.at[k], p_buf.at[k], p_sem.at[k]).wait()

        @pl.when(k == 0)
        def _():
            for s in pair:
                pltpu.make_async_copy(q_all.at[s], q_all.at[s], a_sem.at[s]).wait()

        @pl.when(step == 0)
        def _():
            load_pair((2, 3))

        for later in range(1, RING):
            @pl.when(step == 2 * later - 2)
            def _():
                load_slot(later)

        multiply(k, pair)

    for s in range(SOURCES):
        results[s][...] = outs[s]


def score(info, lists, positive, queries, pieces, extra=()):
    rows, features = queries[0].shape
    flat = list(queries) + [a for arrays in pieces for a in arrays]
    flat += list(extra)
    smem, vmem = pl.BlockSpec(memory_space=pltpu.SMEM), pl.BlockSpec(memory_space=pltpu.VMEM)
    anywhere = pl.BlockSpec(memory_space=pl.ANY)
    stats = [jax.ShapeDtypeStruct((3, rows), jnp.float32)] * SOURCES
    return pl.pallas_call(
        functools.partial(score_kernel, len(extra), float(features) ** -0.5),
        out_shape=stats,
        in_specs=[smem, smem, vmem] + [anywhere] * len(flat),
        out_specs=[vmem] * SOURCES,
        scratch_shapes=[
            pltpu.VMEM((SOURCES, 3, rows), jnp.float32),
            pltpu.VMEM((SOURCES, rows, features), jnp.bfloat16),
            pltpu.VMEM((RING, 2 * PBLK, features), jnp.bfloat16),
            pltpu.SemaphoreType.DMA((SOURCES,)),
            pltpu.SemaphoreType.DMA((RING,)),
        ],
        compiler_params=pltpu.CompilerParams(vmem_limit_bytes=48 * 1024 * 1024),
        cost_estimate=pl.CostEstimate(flops=1000000, bytes_accessed=0, transcendentals=0),
    )(info, lists, positive, *flat)


def finish(stats):
    top, total, chosen = stats[:, 0], stats[:, 1], stats[:, 2]
    peak = jnp.max(top, axis=0)
    summed = jnp.sum(total * jnp.exp(top - peak[None, :]), axis=0)
    return peak + jnp.log(summed) - jnp.sum(chosen, axis=0)


def body(queries, passages, lists, positive):
    info = jnp.stack([lax.axis_index(a) for a in AXES]).astype(jnp.int32)

    size, slots = positive.shape[0], lists.size
    meta = jnp.pad(positive, (0, slots)) + jnp.pad(lists.reshape(-1), (size, 0))
    ahead, behind = shift_x(queries, 1), shift_x(queries, -1)
    ahead = after(ahead, [token([behind], PACE_B)])
    far = shift_x(ahead, 1)
    meta_a = shift_x(meta, 1)
    meta_f = shift_x(meta_a, 1)
    meta_b = shift_x(meta_f, 1)

    s = jnp.stack([passages] + [shift_zy(passages, True, step) for step in (1, -1, 2)])
    s = after(s, [token([meta_f], PACE_M)])
    pr, pl_ = shift_zy(s, False, 1), shift_zy(s, False, -1)
    sides = [both(s)]
    gate = token([sides[0][1], meta_b], PACE_A)
    fr = shift_zy(take(pr, 0, [gate]), False, 1)
    fl = shift_zy(take(pl_, 2, [gate]), False, -1)
    sides += [both(a) for a in (pr, pl_, fr, fl)]
    pieces = [[a for a, _ in sides], [b for _, b in sides]]

    metas = [meta, meta_a, meta_b, meta_f]
    wanted = jnp.stack([m[None, :size] for m in metas])
    ids = jnp.stack([m[size:] for m in metas])
    info = after(info, [token([far], PACE_F)])
    stats = score(info, ids, wanted, [queries, ahead, behind, far], pieces)
    back = [shift_x(a, step) for a, step in zip(stats[1:], (-1, 1, 2))]
    return finish(jnp.stack([stats[0]] + back))


def solution(mesh):
    fine = Mesh(mesh.devices.reshape(RING, 2, RING, RING), AXES)
    everywhere = ("z", "core", "y", "x")
    return jax.shard_map(
        body,
        mesh=fine,
        in_specs=(
            P(everywhere, None),
            P(("y", "x"), ("z", "core")),
            P(everywhere, None),
            P(everywhere),
        ),
        out_specs=P(everywhere),
        check_vma=False,
    )
```

```python
import functools

import jax
import jax.numpy as jnp
from jax import lax
from jax.experimental import pallas as pl
from jax.experimental.pallas import tpu as pltpu
from jax.sharding import Mesh
from jax.sharding import PartitionSpec as P

QROWS = 128
PBLK = 256
LISTED = 8
SOURCES = 4
PIECES = 5
RING = 4
PACE_F = 2
PACE_M, PACE_A, PACE_B = 3, 5, 8
AXES = ("z", "core", "y", "x")
VMEM = 8 * 1024 * 1024
REL = (0, -1, 1, 2)


def ring(axis, step):
    return [(i, (i + step) % RING) for i in range(RING)]


def shift(array, axis, step):
    return lax.ppermute(array, axis, ring(axis, step))


def device(z, core, y, x):
    return ((z * 2 + core) * RING + y) * RING + x


def shift_zy(array, first, step):
    pairs = []
    for z in range(RING):
        for core in range(2):
            for y in range(RING):
                for x in range(RING):
                    along_z = (core == 0) == first
                    to_z = (z + step) % RING if along_z else z
                    to_y = y if along_z else (y + step) % RING
                    pairs.append((device(z, core, y, x), device(to_z, core, to_y, x)))
    return lax.ppermute(array, AXES, pairs)


def shift_x(array, step):
    pairs = []
    for core in range(2):
        for x in range(RING):
            pairs.append((core * RING + x, core * RING + (x + (1 - 2 * core) * step) % RING))
    return lax.ppermute(array, ("core", "x"), pairs)


def both(array):
    return array, swap(array)


def swap(array):
    return lax.ppermute(array, "core", [(0, 1), (1, 0)])


def token(arrays, us):
    def kernel(*refs):
        refs[-1][...] = jnp.zeros_like(refs[-1])

    return pl.pallas_call(
        kernel,
        out_shape=jax.ShapeDtypeStruct((8, 128), jnp.float32),
        in_specs=[pl.BlockSpec(memory_space=pl.ANY)] * len(arrays),
        out_specs=pl.BlockSpec(memory_space=pltpu.VMEM),
        compiler_params=pltpu.CompilerParams(vmem_limit_bytes=VMEM),
        cost_estimate=pl.CostEstimate(
            flops=int(us * 1.15e9), bytes_accessed=0, transcendentals=0
        ),
    )(*arrays)


def after(array, tokens):
    def kernel(*refs):
        pass

    anywhere = pl.BlockSpec(memory_space=pl.ANY)
    return pl.pallas_call(
        kernel,
        out_shape=jax.ShapeDtypeStruct(array.shape, array.dtype),
        in_specs=[anywhere] * (1 + len(tokens)),
        out_specs=anywhere,
        input_output_aliases={0: 0},
        compiler_params=pltpu.CompilerParams(vmem_limit_bytes=VMEM),
        cost_estimate=pl.CostEstimate(flops=1000, bytes_accessed=0, transcendentals=0),
    )(array, *tokens)


def take(array, start, tokens):
    def kernel(ref, *refs):
        out, buf, sems = refs[-3:]
        loads, stores = [], []
        for n in range(2):
            loads.append(pltpu.make_async_copy(ref.at[start + n], buf.at[n], sems.at[n]))
            stores.append(pltpu.make_async_copy(buf.at[n], out.at[n], sems.at[2 + n]))
            loads[n].start()
        for n in range(2):
            loads[n].wait()
            stores[n].start()
        for n in range(2):
            stores[n].wait()

    anywhere = pl.BlockSpec(memory_space=pl.ANY)
    return pl.pallas_call(
        kernel,
        out_shape=jax.ShapeDtypeStruct((2, *array.shape[1:]), array.dtype),
        in_specs=[anywhere] * (1 + len(tokens)),
        out_specs=anywhere,
        scratch_shapes=[pltpu.VMEM((2, *array.shape[1:]), array.dtype), pltpu.SemaphoreType.DMA((4,))],
        compiler_params=pltpu.CompilerParams(vmem_limit_bytes=VMEM),
        cost_estimate=pl.CostEstimate(flops=1000, bytes_accessed=0, transcendentals=0),
    )(array, *tokens)


def score_kernel(extra, scale, info, lists, positive, *refs):
    refs = list(refs)
    queries = [refs.pop(0) for _ in range(SOURCES)]
    pieces = [[refs.pop(0) for _ in range(PIECES)] for _ in range(2)]
    del refs[:extra]
    results = [refs.pop(0) for _ in range(SOURCES)]
    outs, q_all, p_buf, a_sem, p_sem = refs
    me_z, me_core, me_y, me_x = (info[k] for k in range(4))
    feats = p_buf.shape[2] // 8

    def turn(value, step):
        return lax.rem(value + step + RING, RING)

    def any_of(s, block, test):
        found = test(lists[s, block * LISTED])
        for n in range(1, LISTED):
            found = jnp.logical_or(found, test(lists[s, block * LISTED + n]))
        return found

    def load_passages(k, source):
        g = lax.rem(me_core + source, 2)
        for which in range(2):
            @pl.when(g == which)
            def _():
                for m in range(RING):
                    i, j = (k, m) if source == 0 else (m, k)
                    column = pl.multiple_of((turn(me_z, REL[m]) * 2 + source) * feats, feats)
                    n, at = (i, j) if i < 3 else (3 + j // 2, j % 2)
                    pltpu.make_async_copy(
                        pieces[which][n].at[at], p_buf.at[k, :, pl.ds(column, feats)], p_sem.at[k]
                    ).start()

    def load_slot(k):
        for source in range(2):
            load_passages(k, source)

    def load_pair(pair):
        for s in pair:
            pltpu.make_async_copy(queries[s], q_all.at[s], a_sem.at[s]).start()

    load_slot(0)
    load_pair((0, 1))

    def owner_of(k):
        return turn(me_y, jnp.where(k == 3, 2, jnp.where(k == 2, 1, -k))) * RING + me_x

    def choose(k, s):
        owner = owner_of(k)
        block = any_of(s, 1, lambda b: lax.shift_right_arithmetic(b, 1) == owner)
        block = block.astype(jnp.int32)
        return block, pl.ds(pl.multiple_of(block * QROWS, QROWS), QROWS)

    rows = lax.broadcasted_iota(jnp.int32, outs.shape, 1)
    outs[...] = jnp.where(rows == 0, -1e30, 0.0).astype(jnp.float32)
    def multiply(k, pair):
        index = lax.broadcasted_iota(jnp.int32, (PBLK, 2 * QROWS), 0)
        left = lax.broadcasted_iota(jnp.int32, (1, 2 * QROWS), 1) < QROWS
        owner = owner_of(k)
        chosen, lanes = zip(*[choose(k, s) for s in pair])
        listed = []
        for b in range(2):
            sides = [
                any_of(s, block, lambda v: v == owner * 2 + b).astype(jnp.int32)
                for s, block in zip(pair, chosen)
            ]
            listed.append(jnp.where(left, sides[0], sides[1]) > 0)
        rows = jnp.concatenate([q_all[s, part, :] for s, part in zip(pair, lanes)], axis=0)
        scores = lax.dot_general(
            p_buf[k], rows, (((1,), (1,)), ((), ())), preferred_element_type=jnp.float32
        ) * scale

        def get(row):
            found = [outs[s, row : row + 1, part] for s, part in zip(pair, lanes)]
            return jnp.concatenate(found, axis=1)

        wanted = jnp.concatenate(
            [positive[s, :, part] for s, part in zip(pair, lanes)], axis=1
        )
        old = get(0)
        halves = [scores[:PBLK], scores[PBLK:]]
        top = old
        for b in range(2):
            peak = jnp.max(halves[b], axis=0, keepdims=True)
            top = jnp.where(listed[b], jnp.maximum(top, peak), top)
        total = get(1) * jnp.exp(old - top)
        hits = get(2)
        for b in range(2):
            here = jnp.sum(jnp.exp(halves[b] - top), axis=0, keepdims=True)
            total = total + jnp.where(listed[b], here, 0.0)
            place = wanted - (owner * 2 + b) * PBLK
            hits = hits + jnp.sum(jnp.where(index == place, halves[b], 0.0), axis=0, keepdims=True)
        for n, (s, part) in enumerate(zip(pair, lanes)):
            side = slice(n * QROWS, (n + 1) * QROWS)
            outs[s, 0:1, part] = top[:, side]
            outs[s, 1:2, part] = total[:, side]
            outs[s, 2:3, part] = hits[:, side]

    @pl.loop(0, 2 * RING)
    def _(step):
        k, second = step // 2, lax.rem(step, 2)
        pair = (second * 2, second * 2 + 1)

        @pl.when(second == 0)
        def _():
            pltpu.make_async_copy(p_buf.at[k], p_buf.at[k], p_sem.at[k]).wait()

        @pl.when(k == 0)
        def _():
            for s in pair:
                pltpu.make_async_copy(q_all.at[s], q_all.at[s], a_sem.at[s]).wait()

        @pl.when(step == 0)
        def _():
            load_pair((2, 3))

        for later in range(1, RING):
            @pl.when(step == 2 * later - 2)
            def _():
                load_slot(later)

        multiply(k, pair)

    for s in range(SOURCES):
        results[s][...] = outs[s]


def score(info, lists, positive, queries, pieces, extra=()):
    rows, features = queries[0].shape
    flat = list(queries) + [a for arrays in pieces for a in arrays]
    flat += list(extra)
    smem, vmem = pl.BlockSpec(memory_space=pltpu.SMEM), pl.BlockSpec(memory_space=pltpu.VMEM)
    anywhere = pl.BlockSpec(memory_space=pl.ANY)
    stats = [jax.ShapeDtypeStruct((3, rows), jnp.float32)] * SOURCES
    return pl.pallas_call(
        functools.partial(score_kernel, len(extra), float(features) ** -0.5),
        out_shape=stats,
        in_specs=[smem, smem, vmem] + [anywhere] * len(flat),
        out_specs=[vmem] * SOURCES,
        scratch_shapes=[
            pltpu.VMEM((SOURCES, 3, rows), jnp.float32),
            pltpu.VMEM((SOURCES, rows, features), jnp.bfloat16),
            pltpu.VMEM((RING, 2 * PBLK, features), jnp.bfloat16),
            pltpu.SemaphoreType.DMA((SOURCES,)),
            pltpu.SemaphoreType.DMA((RING,)),
        ],
        compiler_params=pltpu.CompilerParams(vmem_limit_bytes=48 * 1024 * 1024),
        cost_estimate=pl.CostEstimate(flops=1000000, bytes_accessed=0, transcendentals=0),
    )(info, lists, positive, *flat)


def finish(stats):
    top, total, chosen = stats[:, 0], stats[:, 1], stats[:, 2]
    peak = jnp.max(top, axis=0)
    summed = jnp.sum(total * jnp.exp(top - peak[None, :]), axis=0)
    return peak + jnp.log(summed) - jnp.sum(chosen, axis=0)


def body(queries, passages, lists, positive):
    info = jnp.stack([lax.axis_index(a) for a in AXES]).astype(jnp.int32)

    size, slots = positive.shape[0], lists.size
    meta = jnp.pad(positive, (0, slots)) + jnp.pad(lists.reshape(-1), (size, 0))
    ahead, behind = shift_x(queries, 1), shift_x(queries, -1)
    ahead = after(ahead, [token([behind], PACE_B)])
    far = shift_x(ahead, 1)
    meta_a = shift_x(meta, 1)
    meta_f = shift_x(meta_a, 1)
    meta_b = shift_x(meta_f, 1)

    s = jnp.stack([passages] + [shift_zy(passages, True, step) for step in (1, -1, 2)])
    s = after(s, [token([meta_f], PACE_M)])
    pr, pl_ = shift_zy(s, False, 1), shift_zy(s, False, -1)
    sides = [both(s)]
    gate = token([sides[0][1], meta_b], PACE_A)
    fr = shift_zy(take(pr, 0, [gate]), False, 1)
    fl = shift_zy(take(pl_, 2, [gate]), False, -1)
    sides += [both(a) for a in (pr, pl_, fr, fl)]
    pieces = [[a for a, _ in sides], [b for _, b in sides]]

    metas = [meta, meta_a, meta_b, meta_f]
    wanted = jnp.stack([m[None, :size] for m in metas])
    ids = jnp.stack([m[size:] for m in metas])
    info = after(info, [token([far], PACE_F)])
    stats = score(info, ids, wanted, [queries, ahead, behind, far], pieces)
    back = [shift_x(a, step) for a, step in zip(stats[1:], (-1, 1, 2))]
    return finish(jnp.stack([stats[0]] + back))


def solution(mesh):
    fine = Mesh(mesh.devices.reshape(RING, 2, RING, RING), AXES)
    everywhere = ("z", "core", "y", "x")
    return jax.shard_map(
        body,
        mesh=fine,
        in_specs=(
            P(everywhere, None),
            P(("y", "x"), ("z", "core")),
            P(everywhere, None),
            P(everywhere),
        ),
        out_specs=P(everywhere),
        check_vma=False,
    )
```
